32 devices in a mesh: grp: 4 (over x, core), seq: 8 (over z, y).
Axes of the slice: x: 2, y: 2, z: 4, core: 2. Of those that a mesh axis runs over, the one named last changes fastest.
Arguments:
- tokens: bfloat16 [8, 512, 1280], P('grp', 'seq'), may hold values from -6 to 6
- lengths: int32 [8], P('grp'), may hold values from 128 to 512, as said below
- query_weight: bfloat16 [1280, 1280], P(('grp', 'seq')), may hold values from -0.15625 to 0.15625
- key_weight: bfloat16 [1280, 1280], P(('grp', 'seq')), may hold values from -0.15625 to 0.15625
- value_weight: bfloat16 [1280, 1280], P(('grp', 'seq')), may hold values from -0.15625 to 0.15625
- out_weight: bfloat16 [1280, 1280], P(('grp', 'seq')), may hold values from -0.5 to 0.5
- up_weight: bfloat16 [1280, 1280], P(('grp', 'seq')), may hold values from -0.15625 to 0.15625
- down_weight: bfloat16 [1280, 1280], P(('grp', 'seq')), may hold values from -0.15625 to 0.15625
- norm_gain: bfloat16 [1280], P(('grp', 'seq')), may hold values from 0.099609375 to 1.8984375
- ff_gain: bfloat16 [1280], P(('grp', 'seq')), may hold values from 0.099609375 to 1.8984375
- up_bias: bfloat16 [1280], P(('grp', 'seq')), may hold values from -3 to 3
- down_bias: bfloat16 [1280], P(('grp', 'seq')), may hold values from -3 to 3
- query_scale: float32 [80], replicated, may hold values from -1 to 1
- cotangent: bfloat16 [8, 512, 1280], P('grp', 'seq'), may hold values from -6 to 6
Outputs:
- activations: bfloat16 [8, 512, 1280], P('grp', 'seq')
- grad_tokens: float32 [8, 512, 1280], P('grp', 'seq')
- grad_query_weight: float32 [1280, 1280], P('seq')
- grad_key_weight: float32 [1280, 1280], P('seq')
- grad_value_weight: float32 [1280, 1280], P('seq')
- grad_out_weight: float32 [1280, 1280], P('seq')
- grad_up_weight: float32 [1280, 1280], P('seq')
- grad_down_weight: float32 [1280, 1280], P('seq')
- grad_norm_gain: float32 [1280], replicated
- grad_ff_gain: float32 [1280], replicated
- grad_up_bias: float32 [1280], replicated
- grad_down_bias: float32 [1280], replicated
- grad_query_scale: float32 [80], replicated
The draws below stay inside these ranges and needn't reach their ends.
Inputs may be any that keep to these rules, and one draw needn't show every extreme that they name: `lengths`: on each index of grp, one of its 2 sequences has all 512 tokens valid.
All inputs are finite; a program needn't handle non-finite values.
Results may differ from the reference program's by a relative error of at most 0.014.
Values may be sent and summed in bfloat16 or wider, within the bound.
No kernel may reach another device: no remote copies, remote signals or barrier semaphores. Data moves between devices by JAX's collectives and lax.ppermute only.
A program may use at most 192 MiB of HBM per device.

```python
import math
import jax
import jax.numpy as jnp
from jax import lax

D = 1280
FF = 1280
HEADS = 16
HD = 80
SEQ_GRP = 2
LEN = 512
SEQS = 8


def draw_lengths(key, part):
    key = jax.random.fold_in(key, 11)
    first_key, second_key = jax.random.split(key)
    drawn = jax.random.randint(first_key, (SEQS,), LEN // 4, LEN + 1, dtype=jnp.int32)
    chosen = jax.random.randint(second_key, (SEQS // SEQ_GRP,), 0, SEQ_GRP, dtype=jnp.int32)
    within = jnp.arange(SEQS, dtype=jnp.int32) % SEQ_GRP
    return jnp.where(within == jnp.repeat(chosen, SEQ_GRP), LEN, drawn).astype(jnp.int32)


def levels(key, shape, pieces, least, high):
    def one(dim, shards_of):
        steps = jax.random.uniform(jax.random.fold_in(jax.random.fold_in(key, 6), dim), (shards_of,), jnp.float32, least / len(pieces), high / len(pieces))
        return jnp.repeat(jnp.exp(steps), shape[dim] // shards_of).reshape((-1,) + (1,) * (len(shape) - dim - 1))

    level = one(*pieces[0])
    for cut in pieces[1:]:
        level = level * one(*cut)
    return level


def normal_values(stream_key, dims, width, bound, cuts=(), kind=jnp.bfloat16):
    values = width * jax.random.normal(stream_key, dims, jnp.float32)
    if cuts:
        values = values * levels(stream_key, dims, cuts, -0.22, 0.18)
    return jnp.clip(values, -bound, bound).astype(kind)


def setup_inputs(seed: int = 0) -> dict:
    seeds = jax.random.split(jax.random.key(seed), 15)
    return {
        "tokens": normal_values(seeds[0], (SEQS, LEN, D), 1.0, 6.0, ((0, 4), (1, 8))),
        "lengths": draw_lengths(jax.random.fold_in(seeds[14], 71), 0),
        "query_weight": normal_values(seeds[2], (D, D), D ** -0.5, 0.15625, ((0, 32),)),
        "key_weight": normal_values(seeds[3], (D, D), D ** -0.5, 0.15625, ((0, 32),)),
        "value_weight": normal_values(seeds[4], (D, D), D ** -0.5, 0.15625, ((0, 32),)),
        "out_weight": normal_values(seeds[5], (D, D), (max(1, 64 * D // LEN)) ** -0.5, 0.5, ((0, 32),)),
        "up_weight": normal_values(seeds[6], (D, FF), D ** -0.5, 0.15625, ((0, 32),)),
        "down_weight": normal_values(seeds[7], (FF, D), FF ** -0.5, 0.15625, ((0, 32),)),
        "norm_gain": jnp.clip(1.0 + 0.18 * jax.random.normal(seeds[8], (D,), jnp.float32), 0.099609375, 1.8984375).astype(jnp.bfloat16),
        "ff_gain": jnp.clip(1.0 + 0.18 * jax.random.normal(seeds[9], (D,), jnp.float32), 0.099609375, 1.8984375).astype(jnp.bfloat16),
        "up_bias": normal_values(seeds[10], (FF,), 0.5, 3.0, ((0, 32),)),
        "down_bias": normal_values(seeds[11], (D,), 0.5, 3.0, ((0, 32),)),
        "query_scale": jnp.clip(jax.random.uniform(seeds[12], (HD,), jnp.float32, -1.0, 1.0), -1.0, 1.0),
        "cotangent": normal_values(seeds[13], (SEQS, LEN, D), 1.0, 6.0, ((0, 4), (1, 8))),
    }


@jax.custom_vjp
def low(v):
    return lax.optimization_barrier(v.astype(jnp.bfloat16)).astype(jnp.float32)

@jax.custom_vjp
def low_back(v):
    return v

def low_keep(v):
    return (low(v), None)

def low_pass(kept, grad):
    return (grad,)

def back_keep(v):
    return (v, None)

def back_low(kept, grad):
    return (low(grad),)
low.defvjp(low_keep, low_pass)
low_back.defvjp(back_keep, back_low)
EPS = 1e-06
QCONST = 1.442695041
NEG = -1e+30
HIGH = lax.Precision.HIGHEST

def product(left, right):
    return jnp.dot(left, right, precision=HIGH, preferred_element_type=jnp.float32)

def inverse_rms(value):
    return lax.rsqrt(lax.optimization_barrier(jnp.mean(value * value, axis=-1, keepdims=True)) + EPS)

def attend(queries, keys, values, length):
    total = queries.shape[0]
    block = math.gcd(total, 512)
    key_pos = jnp.arange(total).astype(jnp.int32)

    def one_block(start):
        query_block = lax.dynamic_slice_in_dim(queries, start, block, 0)
        scores = jnp.einsum('qhe,khe->hqk', query_block, keys, precision=HIGH)
        query_pos = start + jnp.arange(block).astype(jnp.int32)
        allowed = (key_pos[None, :] <= query_pos[:, None]) & (key_pos[None, :] < length)
        scores = low_back(jnp.where(allowed[None], scores, NEG))
        probs = low(jnp.exp(scores - jax.nn.logsumexp(scores, axis=-1, keepdims=True)))
        return jnp.einsum('hqk,khe->qhe', probs, values, precision=HIGH)
    starts = (jnp.arange(total // block) * block).astype(jnp.int32)
    result = lax.map(jax.checkpoint(one_block), starts)
    return result.reshape(total, queries.shape[1], queries.shape[2])

def layer(inputs, query_weight, key_weight, value_weight, out_weight, up_weight, down_weight, norm_gain, ff_gain, up_bias, down_bias, query_scale, lengths):
    scale = QCONST / jnp.sqrt(jnp.float32(HD)) * jax.nn.softplus(query_scale)

    def one_sequence(carry, item):
        tokens, length = item
        normed = low(tokens * inverse_rms(tokens) * norm_gain)
        query_raw = low_back(product(normed, query_weight)).reshape(LEN, HEADS, HD)
        queries = low(low_back(query_raw * scale))
        keys = low(low_back(product(normed, key_weight))).reshape(LEN, HEADS, HD)
        values = low(low_back(product(normed, value_weight))).reshape(LEN, HEADS, HD)
        attended = low(low_back(attend(queries, keys, values, length).reshape(LEN, D)))
        hidden = tokens + low_back(product(attended, out_weight))
        normed_two = low(hidden * inverse_rms(hidden) * ff_gain)
        pre = low_back(product(normed_two, up_weight) + up_bias)
        act = low(jax.nn.silu(pre))
        return (carry, hidden + product(act, down_weight) + down_bias)
    _, result = lax.scan(jax.checkpoint(one_sequence), jnp.float32(0.0), (inputs, lengths))
    return result

def reference(tokens, lengths, query_weight, key_weight, value_weight, out_weight, up_weight, down_weight, norm_gain, ff_gain, up_bias, down_bias, query_scale, cotangent):
    floats = (tokens.astype(jnp.float32), query_weight.astype(jnp.float32), key_weight.astype(jnp.float32), value_weight.astype(jnp.float32), out_weight.astype(jnp.float32), up_weight.astype(jnp.float32), down_weight.astype(jnp.float32), norm_gain.astype(jnp.float32), ff_gain.astype(jnp.float32), up_bias.astype(jnp.float32), down_bias.astype(jnp.float32), query_scale.astype(jnp.float32))

    def forward(*values):
        return layer(*values, lengths)
    result, pullback = jax.vjp(forward, *floats)
    valid = (jnp.arange(LEN).astype(jnp.int32)[None, :] < lengths[:, None]).astype(jnp.float32)
    grads = pullback(cotangent.astype(jnp.float32) * valid[:, :, None])
    return (result.astype(jnp.bfloat16), grads[0], grads[1], grads[2], grads[3], grads[4], grads[5], grads[6], grads[7], grads[8], grads[9], grads[10], grads[11])
```

```python
import math

import jax
import jax.numpy as jnp
from jax import lax
from jax.sharding import PartitionSpec as P

EPS = 1e-06
QCONST = 1.442695041
NEG = -1e30


def heads_of(array, head_size):
    return array.reshape(array.shape[0], array.shape[1], array.shape[2] // head_size, head_size)


def masked_scores(query_rows, query_pos, key_rows, key_pos, lengths, head_size):
    scores = jnp.einsum(
        "sqhe,skhe->shqk",
        heads_of(query_rows, head_size),
        heads_of(key_rows, head_size),
        preferred_element_type=jnp.float32,
    )
    allowed = (key_pos[None, None, :] <= query_pos[None, :, None]) & (
        key_pos[None, None, :] < lengths[:, None, None]
    )
    allowed = allowed[:, None]
    return (jnp.where(allowed, scores, NEG), allowed)


def over_blocks(carry, pieces, update):
    count = pieces[0].shape[1]
    block = math.gcd(count, 512)

    def inner(state, number):
        offset = number * block
        parts = tuple((lax.dynamic_slice_in_dim(piece, offset, block, 1) for piece in pieces))
        return (update(state, parts, offset), None)

    carry, _ = lax.scan(inner, carry, jnp.arange(count // block, dtype=jnp.int32))
    return carry


def shards(
    tokens,
    lengths,
    query_weight,
    key_weight,
    value_weight,
    out_weight,
    up_weight,
    down_weight,
    norm_gain,
    ff_gain,
    up_bias,
    down_bias,
    query_scale,
    cotangent,
):
    seq_count, rows, width = tokens.shape
    head_size = query_scale.shape[0]
    heads = width // head_size
    first = lax.axis_index("seq") * rows
    own_pos = first + jnp.arange(rows, dtype=jnp.int32)
    last_pos = first + rows - 1
    longest = jnp.max(lengths)
    params = (
        query_weight,
        key_weight,
        value_weight,
        out_weight,
        up_weight,
        down_weight,
        norm_gain,
        ff_gain,
        up_bias,
        down_bias,
    )
    whole = (
        lax.all_gather(params[0], ("grp", "seq"), axis=0, tiled=True),
        lax.all_gather(params[1], ("grp", "seq"), axis=0, tiled=True),
        lax.all_gather(params[2], ("grp", "seq"), axis=0, tiled=True),
        lax.all_gather(params[3], ("grp", "seq"), axis=0, tiled=True),
        lax.all_gather(params[4], ("grp", "seq"), axis=0, tiled=True),
        lax.all_gather(params[5], ("grp", "seq"), axis=0, tiled=True),
        lax.all_gather(params[6], ("grp", "seq"), axis=0, tiled=True),
        lax.all_gather(params[7], ("grp", "seq"), axis=0, tiled=True),
        lax.all_gather(params[8], ("grp", "seq"), axis=0, tiled=True),
        lax.all_gather(params[9], ("grp", "seq"), axis=0, tiled=True),
    )
    w_query, w_key, w_value, w_out, w_up, w_down, gain_one, gain_two, bias_up, bias_down = whole
    factor = QCONST / math.sqrt(head_size)
    scale = factor * jax.nn.softplus(query_scale)
    inputs = tokens.astype(jnp.float32)
    inv_one = lax.rsqrt(jnp.mean(inputs * inputs, axis=-1, keepdims=True) + EPS)
    normed = (inputs * inv_one * gain_one.astype(jnp.float32)).astype(jnp.bfloat16)
    query_raw = jnp.einsum("sre,ef->srf", normed, w_query, preferred_element_type=jnp.float32)
    queries = (
        (heads_of(query_raw, head_size) * scale)
        .astype(jnp.bfloat16)
        .reshape(seq_count, rows, width)
    )
    keys = jnp.einsum("sre,ef->srf", normed, w_key, preferred_element_type=jnp.float32).astype(
        jnp.bfloat16
    )
    values = jnp.einsum("sre,ef->srf", normed, w_value, preferred_element_type=jnp.float32).astype(
        jnp.bfloat16
    )

    def peak_update(state, parts, start):
        key_part = parts[0]
        live = (start <= last_pos) & (start < longest)

        def peak_work(current):
            peak, total = current
            key_pos = start + jnp.arange(key_part.shape[1], dtype=jnp.int32)
            scores, allowed = masked_scores(queries, own_pos, key_part, key_pos, lengths, head_size)
            fresh = jnp.maximum(peak, jnp.max(scores, axis=-1))
            weights = jnp.where(allowed, jnp.exp(scores - fresh[..., None]), 0.0)
            return (fresh, total * jnp.exp(peak - fresh) + jnp.sum(weights, axis=-1))

        return lax.cond(live, peak_work, lambda current: current, state)

    stat_shape = (seq_count, heads, rows)
    peak, total = over_blocks(
        (jnp.full(stat_shape, NEG, jnp.float32), jnp.zeros(stat_shape, jnp.float32)),
        (lax.all_gather(keys, "seq", axis=1, tiled=True),),
        peak_update,
    )
    log_total = peak + jnp.log(total)

    def value_update(state, parts, start):
        key_part, value_part = parts
        live = (start <= last_pos) & (start < longest)

        def value_work(current):
            summed, remainder = current
            key_pos = start + jnp.arange(key_part.shape[1], dtype=jnp.int32)
            scores, allowed = masked_scores(queries, own_pos, key_part, key_pos, lengths, head_size)
            probs = jnp.where(allowed, jnp.exp(scores - log_total[..., None]), 0.0)
            rounded = probs.astype(jnp.bfloat16)
            leftover = (probs - rounded.astype(jnp.float32)).astype(jnp.bfloat16)
            value_heads = heads_of(value_part, head_size)
            summed = summed + jnp.einsum(
                "shqk,skhe->sqhe", rounded, value_heads, preferred_element_type=jnp.float32
            )
            remainder = remainder + jnp.einsum(
                "shqk,skhe->sqhe", leftover, value_heads, preferred_element_type=jnp.float32
            )
            return (summed, remainder)

        return lax.cond(live, value_work, lambda current: current, state)

    zero_heads = jnp.zeros((seq_count, rows, heads, head_size), jnp.float32)
    summed, remainder = over_blocks(
        (zero_heads, zero_heads),
        (
            lax.all_gather(keys, "seq", axis=1, tiled=True),
            lax.all_gather(values, "seq", axis=1, tiled=True),
        ),
        value_update,
    )
    attended = summed.reshape(seq_count, rows, width).astype(jnp.bfloat16)
    exact = summed + remainder
    mixed = jnp.einsum("srf,fe->sre", attended, w_out, preferred_element_type=jnp.float32)
    hidden = inputs + mixed
    inv_two = lax.rsqrt(jnp.mean(hidden * hidden, axis=-1, keepdims=True) + EPS)
    normed_two = (hidden * inv_two * gain_two.astype(jnp.float32)).astype(jnp.bfloat16)
    pre = jnp.einsum(
        "sre,ef->srf", normed_two, w_up, preferred_element_type=jnp.float32
    ) + bias_up.astype(jnp.float32)
    act = jax.nn.silu(pre).astype(jnp.bfloat16)
    branch = jnp.einsum("srf,fe->sre", act, w_down, preferred_element_type=jnp.float32)
    layer_out = (hidden + branch + bias_down.astype(jnp.float32)).astype(jnp.bfloat16)
    back = (
        lax.all_gather(params[0], ("grp", "seq"), axis=0, tiled=True),
        lax.all_gather(params[1], ("grp", "seq"), axis=0, tiled=True),
        lax.all_gather(params[2], ("grp", "seq"), axis=0, tiled=True),
        lax.all_gather(params[3], ("grp", "seq"), axis=0, tiled=True),
        lax.all_gather(params[4], ("grp", "seq"), axis=0, tiled=True),
        lax.all_gather(params[5], ("grp", "seq"), axis=0, tiled=True),
        lax.all_gather(params[6], ("grp", "seq"), axis=0, tiled=True),
        lax.all_gather(params[7], ("grp", "seq"), axis=0, tiled=True),
        lax.all_gather(params[8], ("grp", "seq"), axis=0, tiled=True),
        lax.all_gather(params[9], ("grp", "seq"), axis=0, tiled=True),
    )
    back_query, back_key, back_value, back_out, back_up, back_down, back_gain_one, back_gain_two = (
        back[:8]
    )
    valid = own_pos[None, :] < lengths[:, None]
    grad_out = jnp.where(valid[..., None], cotangent, jnp.zeros_like(cotangent))
    grad_down = jnp.einsum("srf,sre->fe", act, grad_out, preferred_element_type=jnp.float32)
    grad_act = jnp.einsum("sre,fe->srf", grad_out, back_down, preferred_element_type=jnp.float32)
    sigma = jax.nn.sigmoid(pre)
    grad_pre = (grad_act * sigma * (1.0 + pre * (1.0 - sigma))).astype(jnp.bfloat16)
    grad_up = jnp.einsum("sre,srf->ef", normed_two, grad_pre, preferred_element_type=jnp.float32)
    grad_normed_two = jnp.einsum(
        "srf,ef->sre", grad_pre, back_up, preferred_element_type=jnp.float32
    )
    grad_gain_two = jnp.sum(grad_normed_two * hidden * inv_two, axis=(0, 1))
    weighted_two = grad_normed_two * back_gain_two.astype(jnp.float32)
    grad_hidden = (
        grad_out.astype(jnp.float32)
        + inv_two * weighted_two
        - hidden
        * (inv_two * inv_two * inv_two)
        * jnp.mean(weighted_two * hidden, axis=-1, keepdims=True)
    )
    grad_mixed = grad_hidden.astype(jnp.bfloat16)
    grad_out_weight = jnp.einsum(
        "srf,sre->fe", attended, grad_mixed, preferred_element_type=jnp.float32
    )
    grad_att = jnp.einsum(
        "sre,fe->srf", grad_mixed, back_out, preferred_element_type=jnp.float32
    ).astype(jnp.bfloat16)
    grad_att_heads = heads_of(grad_att, head_size)
    delta = jnp.einsum("sqhe,sqhe->shq", grad_att_heads.astype(jnp.float32), exact)
    all_log, all_delta = (
        lax.all_gather(log_total, "seq", axis=2, tiled=True),
        lax.all_gather(delta, "seq", axis=2, tiled=True),
    )

    def query_update(state, parts, start):
        key_part, value_part = parts
        live = (start <= last_pos) & (start < longest)

        def query_work(current):
            key_pos = start + jnp.arange(key_part.shape[1], dtype=jnp.int32)
            scores, allowed = masked_scores(queries, own_pos, key_part, key_pos, lengths, head_size)
            probs = jnp.where(allowed, jnp.exp(scores - log_total[..., None]), 0.0)
            grad_probs = jnp.einsum(
                "sqhe,skhe->shqk",
                grad_att_heads,
                heads_of(value_part, head_size),
                preferred_element_type=jnp.float32,
            )
            grad_scores = (probs * (grad_probs - delta[..., None])).astype(jnp.bfloat16)
            return current + jnp.einsum(
                "shqk,skhe->sqhe",
                grad_scores,
                heads_of(key_part, head_size),
                preferred_element_type=jnp.float32,
            )

        return lax.cond(live, query_work, lambda current: current, state)

    grad_query_sum = over_blocks(
        zero_heads,
        (
            lax.all_gather(keys, "seq", axis=1, tiled=True),
            lax.all_gather(values, "seq", axis=1, tiled=True),
        ),
        query_update,
    )
    grad_queries = grad_query_sum.astype(jnp.bfloat16)
    own_values = heads_of(values, head_size)

    def key_update(state, parts, start):
        query_part, grad_part = parts
        count = query_part.shape[1]
        live = (start + count - 1 >= first) & (first < longest)

        def key_work(current):
            grad_key_sum, grad_value_sum = current
            query_pos = start + jnp.arange(count, dtype=jnp.int32)
            scores, allowed = masked_scores(
                query_part, query_pos, keys, own_pos, lengths, head_size
            )
            log_part = lax.dynamic_slice_in_dim(all_log, start, count, 2)
            delta_part = lax.dynamic_slice_in_dim(all_delta, start, count, 2)
            probs = jnp.where(allowed, jnp.exp(scores - log_part[..., None]), 0.0)
            grad_heads = heads_of(grad_part, head_size)
            grad_value_sum = grad_value_sum + jnp.einsum(
                "shqk,sqhe->skhe",
                probs.astype(jnp.bfloat16),
                grad_heads,
                preferred_element_type=jnp.float32,
            )
            grad_probs = jnp.einsum(
                "sqhe,skhe->shqk", grad_heads, own_values, preferred_element_type=jnp.float32
            )
            grad_scores = (probs * (grad_probs - delta_part[..., None])).astype(jnp.bfloat16)
            grad_key_sum = grad_key_sum + jnp.einsum(
                "shqk,sqhe->skhe",
                grad_scores,
                heads_of(query_part, head_size),
                preferred_element_type=jnp.float32,
            )
            return (grad_key_sum, grad_value_sum)

        return lax.cond(live, key_work, lambda current: current, state)

    grad_key_sum, grad_value_sum = over_blocks(
        (zero_heads, zero_heads),
        (
            lax.all_gather(queries, "seq", axis=1, tiled=True),
            lax.all_gather(grad_att, "seq", axis=1, tiled=True),
        ),
        key_update,
    )
    grad_keys = grad_key_sum.reshape(seq_count, rows, width).astype(jnp.bfloat16)
    grad_values = grad_value_sum.reshape(seq_count, rows, width).astype(jnp.bfloat16)
    grad_queries_wide = grad_queries.astype(jnp.float32)
    grad_scale = (
        jnp.sum(grad_queries_wide * heads_of(query_raw, head_size), axis=(0, 1, 2))
        * factor
        * jax.nn.sigmoid(query_scale)
    )
    grad_query_raw = (
        (grad_queries_wide * scale).astype(jnp.bfloat16).reshape(seq_count, rows, width)
    )
    grad_query_w = jnp.einsum(
        "sre,srf->ef", normed, grad_query_raw, preferred_element_type=jnp.float32
    )
    grad_key_w = jnp.einsum("sre,srf->ef", normed, grad_keys, preferred_element_type=jnp.float32)
    grad_value_w = jnp.einsum(
        "sre,srf->ef", normed, grad_values, preferred_element_type=jnp.float32
    )
    grad_normed = (
        jnp.einsum("srf,ef->sre", grad_query_raw, back_query, preferred_element_type=jnp.float32)
        + jnp.einsum("srf,ef->sre", grad_keys, back_key, preferred_element_type=jnp.float32)
        + jnp.einsum("srf,ef->sre", grad_values, back_value, preferred_element_type=jnp.float32)
    )
    grad_gain_one = jnp.sum(grad_normed * inputs * inv_one, axis=(0, 1))
    weighted_one = grad_normed * back_gain_one.astype(jnp.float32)
    grad_tokens = (
        grad_hidden
        + inv_one * weighted_one
        - inputs
        * (inv_one * inv_one * inv_one)
        * jnp.mean(weighted_one * inputs, axis=-1, keepdims=True)
    )
    grad_bias_up = jnp.sum(grad_pre.astype(jnp.float32), axis=(0, 1))
    grad_bias_down = jnp.sum(grad_out.astype(jnp.float32), axis=(0, 1))
    small = lax.psum(
        (grad_gain_one, grad_gain_two, grad_bias_up, grad_bias_down, grad_scale), ("grp", "seq")
    )
    grads = (grad_query_w, grad_key_w, grad_value_w, grad_out_weight, grad_up, grad_down)
    shares = (
        lax.psum_scatter(grads[0], "seq", scatter_dimension=0, tiled=True),
        lax.psum_scatter(grads[1], "seq", scatter_dimension=0, tiled=True),
        lax.psum_scatter(grads[2], "seq", scatter_dimension=0, tiled=True),
        lax.psum_scatter(grads[3], "seq", scatter_dimension=0, tiled=True),
        lax.psum_scatter(grads[4], "seq", scatter_dimension=0, tiled=True),
        lax.psum_scatter(grads[5], "seq", scatter_dimension=0, tiled=True),
    )
    owned = lax.psum((shares[0], shares[1], shares[2], shares[3], shares[4], shares[5]), "grp")
    return (
        layer_out,
        grad_tokens,
        owned[0],
        owned[1],
        owned[2],
        owned[3],
        owned[4],
        owned[5],
        small[0],
        small[1],
        small[2],
        small[3],
        small[4],
    )


def swap(value, axis, bit, size):
    return lax.ppermute(value, axis, [(i, i ^ bit) for i in range(size)])


def in_order(pieces, index):
    low, high = (index & 1) == 1, (index & 2) == 2
    half = [jnp.where(low, pieces[p ^ 1], pieces[p]) for p in range(4)]
    return [jnp.where(high, half[p ^ 2], half[p]) for p in range(4)]


def pick(array, index, axis):
    return lax.dynamic_index_in_dim(array, index, axis, keepdims=False)


def gather_grp(value, g):
    far = swap(value, "grp", 2, 4)
    return in_order([value, swap(value, "grp", 1, 4), far, swap(far, "grp", 1, 4)], g)


def gather_seq(value, z, y):
    mine = jnp.stack(in_order([value] + [swap(value, "seq", 2 * k, 8) for k in (1, 2, 3)], z))
    other = swap(mine, "seq", 1, 8)
    return jnp.where(y == 0, jnp.stack([mine, other], 1), jnp.stack([other, mine], 1))


def scatter_seq(keep, send, z):
    total = keep.astype(jnp.float32) + swap(send, "seq", 1, 8).astype(jnp.float32)
    low = total.astype(jnp.bfloat16)
    own = pick(total, z, 0)
    for k in (1, 2, 3):
        own = own + swap(pick(low, z ^ k, 0), "seq", 2 * k, 8).astype(jnp.float32)
    return own


def quick(
    tokens,
    lengths,
    query_weight,
    key_weight,
    value_weight,
    out_weight,
    up_weight,
    down_weight,
    norm_gain,
    ff_gain,
    up_bias,
    down_bias,
    query_scale,
    cotangent,
):
    low, wide = jnp.bfloat16, jnp.float32
    seq_count, rows, width = tokens.shape
    head_size = query_scale.shape[0]
    share = width // 8
    own_heads = share // head_size
    total_rows = 8 * rows
    g, s = lax.axis_index("grp"), lax.axis_index("seq")
    x, c, z, y = g // 2, g % 2, s // 2, s % 2
    wrows = query_weight.shape[0]

    def dot(a, b, dims):
        return lax.dot_general(a, b, (dims, ((), ())), preferred_element_type=wide)

    all_tokens = [gather_seq(tokens[i], z, y).reshape(total_rows, width) for i in range(seq_count)]
    smalls = jnp.stack([norm_gain, ff_gain, up_bias, down_bias])
    smalls = jnp.pad(smalls, ((0, 4), (0, 3 * share - wrows)))
    payload = jnp.stack([w.reshape(wrows, 8, share) for w in (query_weight, key_weight, value_weight)], 2)
    payload = payload.reshape(wrows, 8, 3 * share).transpose(1, 0, 2)
    payload = jnp.concatenate([payload, jnp.broadcast_to(smalls, (8,) + smalls.shape)], 1)
    columns = lax.all_to_all(payload, "seq", 0, 0, tiled=True)
    columns = jnp.stack(gather_grp(columns, g))
    w_qkv = columns[:, :, :wrows].reshape(width, 3 * share)
    gains = columns[:, :, wrows : wrows + 4, :wrows].transpose(2, 0, 1, 3).reshape(4, width)
    gain_one, gain_two, bias_up, bias_down = (gains[k].astype(wide) for k in range(4))

    packed = jnp.stack([out_weight, up_weight, down_weight])
    w_out, w_up, w_down = (
        jnp.stack(gather_grp(gather_seq(w, z, y), g)).reshape(width, width)
        for w in (out_weight, up_weight, down_weight)
    )
    factor = QCONST / math.sqrt(head_size)
    scale = factor * jax.nn.softplus(query_scale)
    scale_row = jnp.tile(scale, own_heads)

    position = jnp.arange(total_rows, dtype=jnp.int32)
    causal = position[None, :] <= position[:, None]

    def split(a):
        return a.reshape(total_rows, own_heads, head_size)

    saved, mixed_parts = [], []
    for i in range(seq_count):
        tok = all_tokens[i].astype(wide)
        inv = lax.rsqrt(jnp.mean(tok * tok, axis=-1, keepdims=True) + EPS)
        normed = (tok * inv * gain_one).astype(low)
        qkv = dot(normed, w_qkv, ((1,), (0,)))
        query_raw = qkv[:, :share]
        q = split((query_raw * scale_row).astype(low))
        k = split(qkv[:, share : 2 * share].astype(low))
        v = split(qkv[:, 2 * share :].astype(low))
        allowed = causal & (position[None, :] < lengths[i])
        scores = jnp.einsum("qhe,khe->hqk", q, k, preferred_element_type=wide)
        scores = jnp.where(allowed, scores, NEG)
        probs = jax.nn.softmax(scores, axis=-1)
        att = jnp.einsum("hqk,khe->qhe", probs.astype(low), v, preferred_element_type=wide)
        mixed_parts.append(att.astype(low).reshape(8, rows, share))
        saved.append((tok * inv, normed, query_raw, q, k, v, probs))
    att = lax.all_to_all(jnp.stack(mixed_parts, 1), "seq", 0, 0, tiled=True)
    attended = att.reshape(8, seq_count * rows, share).transpose(1, 0, 2).reshape(-1, width)

    inputs = tokens.reshape(-1, width).astype(wide)
    hidden = inputs + dot(attended, w_out, ((1,), (0,)))
    inv_two = lax.rsqrt(jnp.mean(hidden * hidden, axis=-1, keepdims=True) + EPS)
    normed_two = (hidden * inv_two * gain_two).astype(low)
    pre = dot(normed_two, w_up, ((1,), (0,))) + bias_up
    sigma = jax.nn.sigmoid(pre)
    act = (pre * sigma).astype(low)
    layer_out = (hidden + dot(act, w_down, ((1,), (0,))) + bias_down).astype(low)
    own_pos = s * rows + jnp.arange(rows, dtype=jnp.int32)
    valid = own_pos[None, :] < lengths[:, None]
    grad_out = jnp.where(valid[..., None], cotangent, jnp.zeros_like(cotangent)).reshape(-1, width)
    grad_act = dot(grad_out, w_down, ((1,), (1,)))
    grad_pre = (grad_act * sigma * (1.0 + pre * (1.0 - sigma))).astype(low)
    grad_normed_two = dot(grad_pre, w_up, ((1,), (1,)))
    grad_gain_two = jnp.sum(grad_normed_two * hidden * inv_two, axis=0)
    weighted = grad_normed_two * gain_two
    grad_hidden = (
        grad_out.astype(wide)
        + inv_two * weighted
        - hidden * (inv_two * inv_two * inv_two) * jnp.mean(weighted * hidden, axis=-1, keepdims=True)
    )
    grad_mixed = grad_hidden.astype(low)
    grad_att = dot(grad_mixed, w_out, ((1,), (1,))).astype(low)
    grad_att = grad_att.reshape(seq_count * rows, 8, share).transpose(1, 0, 2)
    grad_att = lax.all_to_all(grad_att, "seq", 0, 0, tiled=True).reshape(8, seq_count, rows, share)

    left = jnp.concatenate([attended, normed_two, act], 1)
    right = jnp.stack([grad_mixed, grad_pre, grad_out]).reshape(3, seq_count * rows, 2, width // 2)
    left_two = jnp.concatenate([left, swap(left, "grp", 2, 4)], 0)
    right_two = jnp.concatenate([pick(right, x, 2), swap(pick(right, 1 - x, 2), "grp", 2, 4)], 1)
    right_two = right_two.reshape(3, 2 * seq_count * rows, 2, width // 4)
    left_four = jnp.concatenate([left_two, swap(left_two, "grp", 1, 4)], 0)
    right_four = jnp.concatenate([pick(right_two, c, 2), swap(pick(right_two, 1 - c, 2), "grp", 1, 4)], 1)
    quarter = jnp.stack(
        [dot(left_four[:, k * width : (k + 1) * width], right_four[k], ((0,), (0,))) for k in range(3)]
    )
    quarter = quarter.astype(low).reshape(3, 4, 2, share, width // 4).transpose(2, 1, 0, 3, 4)
    ff_grads = scatter_seq(pick(quarter, y, 0), pick(quarter, 1 - y, 0), z).astype(low)
    ff_grads = jnp.concatenate(gather_grp(ff_grads, g), 2).astype(wide)

    grad_qkv_w = jnp.zeros((width, 3 * share), wide)
    grad_gain_one = jnp.zeros((width,), wide)
    grad_scale = jnp.zeros((head_size,), wide)
    grad_normed = []
    for i in range(seq_count):
        unit, normed, query_raw, q, k, v, probs = saved[i]
        ga = split(grad_att[:, i].reshape(total_rows, share))
        grad_probs = jnp.einsum("qhe,khe->hqk", ga, v, preferred_element_type=wide)
        delta = jnp.sum(grad_probs * probs, axis=-1, keepdims=True)
        grad_scores = (probs * (grad_probs - delta)).astype(low)
        gq = jnp.einsum("hqk,khe->qhe", grad_scores, k, preferred_element_type=wide).astype(low)
        gk = jnp.einsum("hqk,qhe->khe", grad_scores, q, preferred_element_type=wide).astype(low)
        gv = jnp.einsum("hqk,qhe->khe", probs.astype(low), ga, preferred_element_type=wide).astype(low)
        gq_wide = gq.astype(wide)
        grad_scale = grad_scale + jnp.sum(gq_wide * split(query_raw), axis=(0, 1))
        gq = (gq_wide * scale).astype(low)
        grads = jnp.concatenate([a.reshape(total_rows, share) for a in (gq, gk, gv)], 1)
        grad_qkv_w = grad_qkv_w + dot(normed, grads, ((0,), (0,)))
        partial = dot(grads, w_qkv, ((1,), (1,)))
        grad_gain_one = grad_gain_one + jnp.sum(partial * unit, axis=0)
        blocks = partial.astype(low).reshape(4, 2, rows, width)
        grad_normed.append(scatter_seq(pick(blocks, y, 1), pick(blocks, 1 - y, 1), z))
    grad_normed = jnp.concatenate(grad_normed, 0)
    inv_one = lax.rsqrt(jnp.mean(inputs * inputs, axis=-1, keepdims=True) + EPS)
    weighted = grad_normed * gain_one
    grad_tokens = (
        grad_hidden
        + inv_one * weighted
        - inputs * (inv_one * inv_one * inv_one) * jnp.mean(weighted * inputs, axis=-1, keepdims=True)
    )

    halves = grad_qkv_w.astype(low).reshape(8, 2, 2, wrows, 3 * share)
    half = pick(halves, c, 2).astype(wide) + swap(pick(halves, 1 - c, 2), "grp", 1, 4).astype(wide)
    half = half.astype(low)
    part = pick(half, x, 1).astype(wide) + swap(pick(half, 1 - x, 1), "grp", 2, 4).astype(wide)
    part = lax.all_to_all(part.astype(low), "seq", 0, 0, tiled=True)
    qkv_grads = jnp.stack(gather_grp(part, g)).astype(wide).reshape(4, 8, wrows, 3, share)
    qkv_grads = qkv_grads.transpose(3, 0, 2, 1, 4).reshape(3, share, width)

    sums = jnp.stack(
        [
            grad_gain_one,
            grad_gain_two,
            jnp.sum(grad_pre.astype(wide), axis=0),
            jnp.sum(grad_out.astype(wide), axis=0),
            jnp.pad(grad_scale * factor * jax.nn.sigmoid(query_scale), (0, width - head_size)),
        ]
    )
    for axis, bit, size in (("grp", 1, 4), ("grp", 2, 4), ("seq", 1, 8), ("seq", 2, 8), ("seq", 4, 8)):
        sums = sums + swap(sums, axis, bit, size)
    shape = (seq_count, rows, width)
    return (
        layer_out.reshape(shape),
        grad_tokens.reshape(shape),
        qkv_grads[0],
        qkv_grads[1],
        qkv_grads[2],
        ff_grads[0],
        ff_grads[1],
        ff_grads[2],
        sums[0],
        sums[1],
        sums[2],
        sums[3],
        sums[4, :head_size],
    )


def solution(mesh):
    fits = mesh.shape["grp"] == 4 and mesh.shape["seq"] == 8
    return jax.shard_map(
        quick if fits else shards,
        mesh=mesh,
        in_specs=(
            P("grp", "seq", None),
            P("grp"),
            P(("grp", "seq"), None),
            P(("grp", "seq"), None),
            P(("grp", "seq"), None),
            P(("grp", "seq"), None),
            P(("grp", "seq"), None),
            P(("grp", "seq"), None),
            P(("grp", "seq")),
            P(("grp", "seq")),
            P(("grp", "seq")),
            P(("grp", "seq")),
            P(),
            P("grp", "seq", None),
        ),
        out_specs=(
            P("grp", "seq", None),
            P("grp", "seq", None),
            P("seq", None),
            P("seq", None),
            P("seq", None),
            P("seq", None),
            P("seq", None),
            P("seq", None),
            P(),
            P(),
            P(),
            P(),
            P(),
        ),
        check_vma=False,
    )
```

```python
import functools
import math

import jax
import jax.numpy as jnp
from jax import lax
from jax.experimental import pallas as pl
from jax.experimental.pallas import tpu as pltpu
from jax.sharding import PartitionSpec as P

EPS = 1e-06
QCONST = 1.442695041
NEG = -1e30


def heads_of(array, head_size):
    return array.reshape(array.shape[0], array.shape[1], array.shape[2] // head_size, head_size)


def masked_scores(query_rows, query_pos, key_rows, key_pos, lengths, head_size):
    scores = jnp.einsum(
        "sqhe,skhe->shqk",
        heads_of(query_rows, head_size),
        heads_of(key_rows, head_size),
        preferred_element_type=jnp.float32,
    )
    allowed = (key_pos[None, None, :] <= query_pos[None, :, None]) & (
        key_pos[None, None, :] < lengths[:, None, None]
    )
    allowed = allowed[:, None]
    return (jnp.where(allowed, scores, NEG), allowed)


def over_blocks(carry, pieces, update):
    count = pieces[0].shape[1]
    block = math.gcd(count, 512)

    def inner(state, number):
        offset = number * block
        parts = tuple((lax.dynamic_slice_in_dim(piece, offset, block, 1) for piece in pieces))
        return (update(state, parts, offset), None)

    carry, _ = lax.scan(inner, carry, jnp.arange(count // block, dtype=jnp.int32))
    return carry


def shards(
    tokens,
    lengths,
    query_weight,
    key_weight,
    value_weight,
    out_weight,
    up_weight,
    down_weight,
    norm_gain,
    ff_gain,
    up_bias,
    down_bias,
    query_scale,
    cotangent,
):
    seq_count, rows, width = tokens.shape
    head_size = query_scale.shape[0]
    heads = width // head_size
    first = lax.axis_index("seq") * rows
    own_pos = first + jnp.arange(rows, dtype=jnp.int32)
    last_pos = first + rows - 1
    longest = jnp.max(lengths)
    params = (
        query_weight,
        key_weight,
        value_weight,
        out_weight,
        up_weight,
        down_weight,
        norm_gain,
        ff_gain,
        up_bias,
        down_bias,
    )
    whole = (
        lax.all_gather(params[0], ("grp", "seq"), axis=0, tiled=True),
        lax.all_gather(params[1], ("grp", "seq"), axis=0, tiled=True),
        lax.all_gather(params[2], ("grp", "seq"), axis=0, tiled=True),
        lax.all_gather(params[3], ("grp", "seq"), axis=0, tiled=True),
        lax.all_gather(params[4], ("grp", "seq"), axis=0, tiled=True),
        lax.all_gather(params[5], ("grp", "seq"), axis=0, tiled=True),
        lax.all_gather(params[6], ("grp", "seq"), axis=0, tiled=True),
        lax.all_gather(params[7], ("grp", "seq"), axis=0, tiled=True),
        lax.all_gather(params[8], ("grp", "seq"), axis=0, tiled=True),
        lax.all_gather(params[9], ("grp", "seq"), axis=0, tiled=True),
    )
    w_query, w_key, w_value, w_out, w_up, w_down, gain_one, gain_two, bias_up, bias_down = whole
    factor = QCONST / math.sqrt(head_size)
    scale = factor * jax.nn.softplus(query_scale)
    inputs = tokens.astype(jnp.float32)
    inv_one = lax.rsqrt(jnp.mean(inputs * inputs, axis=-1, keepdims=True) + EPS)
    normed = (inputs * inv_one * gain_one.astype(jnp.float32)).astype(jnp.bfloat16)
    query_raw = jnp.einsum("sre,ef->srf", normed, w_query, preferred_element_type=jnp.float32)
    queries = (
        (heads_of(query_raw, head_size) * scale)
        .astype(jnp.bfloat16)
        .reshape(seq_count, rows, width)
    )
    keys = jnp.einsum("sre,ef->srf", normed, w_key, preferred_element_type=jnp.float32).astype(
        jnp.bfloat16
    )
    values = jnp.einsum("sre,ef->srf", normed, w_value, preferred_element_type=jnp.float32).astype(
        jnp.bfloat16
    )

    def peak_update(state, parts, start):
        key_part = parts[0]
        live = (start <= last_pos) & (start < longest)

        def peak_work(current):
            peak, total = current
            key_pos = start + jnp.arange(key_part.shape[1], dtype=jnp.int32)
            scores, allowed = masked_scores(queries, own_pos, key_part, key_pos, lengths, head_size)
            fresh = jnp.maximum(peak, jnp.max(scores, axis=-1))
            weights = jnp.where(allowed, jnp.exp(scores - fresh[..., None]), 0.0)
            return (fresh, total * jnp.exp(peak - fresh) + jnp.sum(weights, axis=-1))

        return lax.cond(live, peak_work, lambda current: current, state)

    stat_shape = (seq_count, heads, rows)
    peak, total = over_blocks(
        (jnp.full(stat_shape, NEG, jnp.float32), jnp.zeros(stat_shape, jnp.float32)),
        (lax.all_gather(keys, "seq", axis=1, tiled=True),),
        peak_update,
    )
    log_total = peak + jnp.log(total)

    def value_update(state, parts, start):
        key_part, value_part = parts
        live = (start <= last_pos) & (start < longest)

        def value_work(current):
            summed, remainder = current
            key_pos = start + jnp.arange(key_part.shape[1], dtype=jnp.int32)
            scores, allowed = masked_scores(queries, own_pos, key_part, key_pos, lengths, head_size)
            probs = jnp.where(allowed, jnp.exp(scores - log_total[..., None]), 0.0)
            rounded = probs.astype(jnp.bfloat16)
            leftover = (probs - rounded.astype(jnp.float32)).astype(jnp.bfloat16)
            value_heads = heads_of(value_part, head_size)
            summed = summed + jnp.einsum(
                "shqk,skhe->sqhe", rounded, value_heads, preferred_element_type=jnp.float32
            )
            remainder = remainder + jnp.einsum(
                "shqk,skhe->sqhe", leftover, value_heads, preferred_element_type=jnp.float32
            )
            return (summed, remainder)

        return lax.cond(live, value_work, lambda current: current, state)

    zero_heads = jnp.zeros((seq_count, rows, heads, head_size), jnp.float32)
    summed, remainder = over_blocks(
        (zero_heads, zero_heads),
        (
            lax.all_gather(keys, "seq", axis=1, tiled=True),
            lax.all_gather(values, "seq", axis=1, tiled=True),
        ),
        value_update,
    )
    attended = summed.reshape(seq_count, rows, width).astype(jnp.bfloat16)
    exact = summed + remainder
    mixed = jnp.einsum("srf,fe->sre", attended, w_out, preferred_element_type=jnp.float32)
    hidden = inputs + mixed
    inv_two = lax.rsqrt(jnp.mean(hidden * hidden, axis=-1, keepdims=True) + EPS)
    normed_two = (hidden * inv_two * gain_two.astype(jnp.float32)).astype(jnp.bfloat16)
    pre = jnp.einsum(
        "sre,ef->srf", normed_two, w_up, preferred_element_type=jnp.float32
    ) + bias_up.astype(jnp.float32)
    act = jax.nn.silu(pre).astype(jnp.bfloat16)
    branch = jnp.einsum("srf,fe->sre", act, w_down, preferred_element_type=jnp.float32)
    layer_out = (hidden + branch + bias_down.astype(jnp.float32)).astype(jnp.bfloat16)
    back = (
        lax.all_gather(params[0], ("grp", "seq"), axis=0, tiled=True),
        lax.all_gather(params[1], ("grp", "seq"), axis=0, tiled=True),
        lax.all_gather(params[2], ("grp", "seq"), axis=0, tiled=True),
        lax.all_gather(params[3], ("grp", "seq"), axis=0, tiled=True),
        lax.all_gather(params[4], ("grp", "seq"), axis=0, tiled=True),
        lax.all_gather(params[5], ("grp", "seq"), axis=0, tiled=True),
        lax.all_gather(params[6], ("grp", "seq"), axis=0, tiled=True),
        lax.all_gather(params[7], ("grp", "seq"), axis=0, tiled=True),
        lax.all_gather(params[8], ("grp", "seq"), axis=0, tiled=True),
        lax.all_gather(params[9], ("grp", "seq"), axis=0, tiled=True),
    )
    back_query, back_key, back_value, back_out, back_up, back_down, back_gain_one, back_gain_two = (
        back[:8]
    )
    valid = own_pos[None, :] < lengths[:, None]
    grad_out = jnp.where(valid[..., None], cotangent, jnp.zeros_like(cotangent))
    grad_down = jnp.einsum("srf,sre->fe", act, grad_out, preferred_element_type=jnp.float32)
    grad_act = jnp.einsum("sre,fe->srf", grad_out, back_down, preferred_element_type=jnp.float32)
    sigma = jax.nn.sigmoid(pre)
    grad_pre = (grad_act * sigma * (1.0 + pre * (1.0 - sigma))).astype(jnp.bfloat16)
    grad_up = jnp.einsum("sre,srf->ef", normed_two, grad_pre, preferred_element_type=jnp.float32)
    grad_normed_two = jnp.einsum(
        "srf,ef->sre", grad_pre, back_up, preferred_element_type=jnp.float32
    )
    grad_gain_two = jnp.sum(grad_normed_two * hidden * inv_two, axis=(0, 1))
    weighted_two = grad_normed_two * back_gain_two.astype(jnp.float32)
    grad_hidden = (
        grad_out.astype(jnp.float32)
        + inv_two * weighted_two
        - hidden
        * (inv_two * inv_two * inv_two)
        * jnp.mean(weighted_two * hidden, axis=-1, keepdims=True)
    )
    grad_mixed = grad_hidden.astype(jnp.bfloat16)
    grad_out_weight = jnp.einsum(
        "srf,sre->fe", attended, grad_mixed, preferred_element_type=jnp.float32
    )
    grad_att = jnp.einsum(
        "sre,fe->srf", grad_mixed, back_out, preferred_element_type=jnp.float32
    ).astype(jnp.bfloat16)
    grad_att_heads = heads_of(grad_att, head_size)
    delta = jnp.einsum("sqhe,sqhe->shq", grad_att_heads.astype(jnp.float32), exact)
    all_log, all_delta = (
        lax.all_gather(log_total, "seq", axis=2, tiled=True),
        lax.all_gather(delta, "seq", axis=2, tiled=True),
    )

    def query_update(state, parts, start):
        key_part, value_part = parts
        live = (start <= last_pos) & (start < longest)

        def query_work(current):
            key_pos = start + jnp.arange(key_part.shape[1], dtype=jnp.int32)
            scores, allowed = masked_scores(queries, own_pos, key_part, key_pos, lengths, head_size)
            probs = jnp.where(allowed, jnp.exp(scores - log_total[..., None]), 0.0)
            grad_probs = jnp.einsum(
                "sqhe,skhe->shqk",
                grad_att_heads,
                heads_of(value_part, head_size),
                preferred_element_type=jnp.float32,
            )
            grad_scores = (probs * (grad_probs - delta[..., None])).astype(jnp.bfloat16)
            return current + jnp.einsum(
                "shqk,skhe->sqhe",
                grad_scores,
                heads_of(key_part, head_size),
                preferred_element_type=jnp.float32,
            )

        return lax.cond(live, query_work, lambda current: current, state)

    grad_query_sum = over_blocks(
        zero_heads,
        (
            lax.all_gather(keys, "seq", axis=1, tiled=True),
            lax.all_gather(values, "seq", axis=1, tiled=True),
        ),
        query_update,
    )
    grad_queries = grad_query_sum.astype(jnp.bfloat16)
    own_values = heads_of(values, head_size)

    def key_update(state, parts, start):
        query_part, grad_part = parts
        count = query_part.shape[1]
        live = (start + count - 1 >= first) & (first < longest)

        def key_work(current):
            grad_key_sum, grad_value_sum = current
            query_pos = start + jnp.arange(count, dtype=jnp.int32)
            scores, allowed = masked_scores(
                query_part, query_pos, keys, own_pos, lengths, head_size
            )
            log_part = lax.dynamic_slice_in_dim(all_log, start, count, 2)
            delta_part = lax.dynamic_slice_in_dim(all_delta, start, count, 2)
            probs = jnp.where(allowed, jnp.exp(scores - log_part[..., None]), 0.0)
            grad_heads = heads_of(grad_part, head_size)
            grad_value_sum = grad_value_sum + jnp.einsum(
                "shqk,sqhe->skhe",
                probs.astype(jnp.bfloat16),
                grad_heads,
                preferred_element_type=jnp.float32,
            )
            grad_probs = jnp.einsum(
                "sqhe,skhe->shqk", grad_heads, own_values, preferred_element_type=jnp.float32
            )
            grad_scores = (probs * (grad_probs - delta_part[..., None])).astype(jnp.bfloat16)
            grad_key_sum = grad_key_sum + jnp.einsum(
                "shqk,sqhe->skhe",
                grad_scores,
                heads_of(query_part, head_size),
                preferred_element_type=jnp.float32,
            )
            return (grad_key_sum, grad_value_sum)

        return lax.cond(live, key_work, lambda current: current, state)

    grad_key_sum, grad_value_sum = over_blocks(
        (zero_heads, zero_heads),
        (
            lax.all_gather(queries, "seq", axis=1, tiled=True),
            lax.all_gather(grad_att, "seq", axis=1, tiled=True),
        ),
        key_update,
    )
    grad_keys = grad_key_sum.reshape(seq_count, rows, width).astype(jnp.bfloat16)
    grad_values = grad_value_sum.reshape(seq_count, rows, width).astype(jnp.bfloat16)
    grad_queries_wide = grad_queries.astype(jnp.float32)
    grad_scale = (
        jnp.sum(grad_queries_wide * heads_of(query_raw, head_size), axis=(0, 1, 2))
        * factor
        * jax.nn.sigmoid(query_scale)
    )
    grad_query_raw = (
        (grad_queries_wide * scale).astype(jnp.bfloat16).reshape(seq_count, rows, width)
    )
    grad_query_w = jnp.einsum(
        "sre,srf->ef", normed, grad_query_raw, preferred_element_type=jnp.float32
    )
    grad_key_w = jnp.einsum("sre,srf->ef", normed, grad_keys, preferred_element_type=jnp.float32)
    grad_value_w = jnp.einsum(
        "sre,srf->ef", normed, grad_values, preferred_element_type=jnp.float32
    )
    grad_normed = (
        jnp.einsum("srf,ef->sre", grad_query_raw, back_query, preferred_element_type=jnp.float32)
        + jnp.einsum("srf,ef->sre", grad_keys, back_key, preferred_element_type=jnp.float32)
        + jnp.einsum("srf,ef->sre", grad_values, back_value, preferred_element_type=jnp.float32)
    )
    grad_gain_one = jnp.sum(grad_normed * inputs * inv_one, axis=(0, 1))
    weighted_one = grad_normed * back_gain_one.astype(jnp.float32)
    grad_tokens = (
        grad_hidden
        + inv_one * weighted_one
        - inputs
        * (inv_one * inv_one * inv_one)
        * jnp.mean(weighted_one * inputs, axis=-1, keepdims=True)
    )
    grad_bias_up = jnp.sum(grad_pre.astype(jnp.float32), axis=(0, 1))
    grad_bias_down = jnp.sum(grad_out.astype(jnp.float32), axis=(0, 1))
    small = lax.psum(
        (grad_gain_one, grad_gain_two, grad_bias_up, grad_bias_down, grad_scale), ("grp", "seq")
    )
    grads = (grad_query_w, grad_key_w, grad_value_w, grad_out_weight, grad_up, grad_down)
    shares = (
        lax.psum_scatter(grads[0], "seq", scatter_dimension=0, tiled=True),
        lax.psum_scatter(grads[1], "seq", scatter_dimension=0, tiled=True),
        lax.psum_scatter(grads[2], "seq", scatter_dimension=0, tiled=True),
        lax.psum_scatter(grads[3], "seq", scatter_dimension=0, tiled=True),
        lax.psum_scatter(grads[4], "seq", scatter_dimension=0, tiled=True),
        lax.psum_scatter(grads[5], "seq", scatter_dimension=0, tiled=True),
    )
    owned = lax.psum((shares[0], shares[1], shares[2], shares[3], shares[4], shares[5]), "grp")
    return (
        layer_out,
        grad_tokens,
        owned[0],
        owned[1],
        owned[2],
        owned[3],
        owned[4],
        owned[5],
        small[0],
        small[1],
        small[2],
        small[3],
        small[4],
    )


LOW, WIDE = jnp.bfloat16, jnp.float32
VMEM_BYTES = 48 * 1024 * 1024


def swap(value, axis, bit, size):
    return lax.ppermute(value, axis, [(i, i ^ bit) for i in range(size)])


def in_order(pieces, index):
    low, high = (index & 1) == 1, (index & 2) == 2
    half = [jnp.where(low, pieces[p ^ 1], pieces[p]) for p in range(4)]
    return [jnp.where(high, half[p ^ 2], half[p]) for p in range(4)]


def over_grp(value):
    far = swap(value, "grp", 2, 4)
    return [value, swap(value, "grp", 1, 4), far, swap(far, "grp", 1, 4)]


def over_z(value, z):
    return jnp.stack(in_order([value] + [swap(value, "seq", 2 * k, 8) for k in (1, 2, 3)], z))


def gather_seq(value, z, y):
    mine = over_z(value, z)
    other = swap(mine, "seq", 1, 8)
    return jnp.where(y == 0, jnp.stack([mine, other], 1), jnp.stack([other, mine], 1))


def nn(a, b):
    return lax.dot_general(a, b, (((1,), (0,)), ((), ())), preferred_element_type=WIDE)


def nt(a, b):
    return lax.dot_general(a, b, (((1,), (1,)), ((), ())), preferred_element_type=WIDE)


def tn(a, b):
    return lax.dot_general(a, b, (((0,), (0,)), ((), ())), preferred_element_type=WIDE)


SMEM = pl.BlockSpec(memory_space=pltpu.SMEM)
VMEM = pl.BlockSpec(memory_space=pltpu.VMEM)
ANY = pl.BlockSpec(memory_space=pl.ANY)


def call(body, outs, ins, scratch=(), flops=0, **more):
    moved = sum(a.size * a.dtype.itemsize for a, _ in ins)
    return pl.pallas_call(
        body,
        out_shape=outs,
        in_specs=[spec for _, spec in ins],
        out_specs=jax.tree.map(lambda _: VMEM, outs),
        scratch_shapes=list(scratch),
        compiler_params=pltpu.CompilerParams(vmem_limit_bytes=VMEM_BYTES),
        cost_estimate=pl.CostEstimate(flops=flops, bytes_accessed=moved, transcendentals=0),
        **more,
    )(*[a for a, _ in ins])


def shape(*dims, dtype=LOW):
    return jax.ShapeDtypeStruct(dims, dtype)


def load_tokens(info, mine, other, x, seq, rows):
    y = info[0]
    for k in range(4):
        x[pl.ds((2 * k + y) * rows, rows), :] = mine[k, seq]
        x[pl.ds((2 * k + 1 - y) * rows, rows), :] = other[k, seq]


def project(x, gain, w):
    wide = x[...].astype(WIDE)
    inv = lax.rsqrt(jnp.mean(wide * wide, axis=-1, keepdims=True) + EPS)
    unit = wide * inv
    normed = (unit * gain[...]).astype(LOW)
    return unit, normed, nn(normed, w[...])


def probabilities(q, k, first, length):
    scores = nt(q, k)
    query = first + lax.broadcasted_iota(jnp.int32, scores.shape, 0)
    key = lax.broadcasted_iota(jnp.int32, scores.shape, 1)
    scores = jnp.where((key <= query) & (key < length), scores, NEG)
    raised = jnp.exp(scores - jnp.max(scores, axis=-1, keepdims=True))
    return raised / jnp.sum(raised, axis=-1, keepdims=True)


def attend_kernel(size, info, mine, other, w, gain, scale, out, x):
    seq_count, rows = mine.shape[1:3]
    share = out.shape[-1]
    total = 8 * rows
    block = total // 2
    for seq in range(seq_count):
        load_tokens(info, mine, other, x, seq, rows)
        _, _, qkv = project(x, gain, w)
        heads = []
        for h in range(share // size):
            at = h * size
            q = (qkv[:, at : at + size] * scale[...]).astype(LOW)
            k = qkv[:, share + at : share + at + size].astype(LOW)
            v = qkv[:, 2 * share + at : 2 * share + at + size].astype(LOW)
            parts = []
            for b in range(2):
                end = (b + 1) * block
                probs = probabilities(q[b * block : end], k[:end], b * block, info[1 + seq])
                parts.append(nn(probs.astype(LOW), v[:end]))
            heads.append(jnp.concatenate(parts, 0))
        att = jnp.concatenate(heads, 1).astype(LOW)
        for t in range(8):
            out[t, seq] = att[t * rows : (t + 1) * rows]


def attend_back_kernel(size, seq, info, mine, other, w, gain, scale, ga, *refs):
    if seq:
        before, sums_before, keep, send, left, right, sums, x, p_ref, g_ref = refs
    else:
        keep, send, grads, sums, x, p_ref = refs
    rows = mine.shape[2]
    share = ga.shape[-1]
    total = 8 * rows
    block = total // 2
    width = x.shape[1]
    y = info[0]
    load_tokens(info, mine, other, x, seq, rows)
    unit, normed, qkv = project(x, gain, w)
    whole = jnp.concatenate([ga[t, seq] for t in range(8)], 0)
    grad_q, grad_k, grad_v, grad_scale = [], [], [], jnp.zeros((1, size), WIDE)
    for h in range(share // size):
        at = h * size
        raw = qkv[:, at : at + size]
        q = (raw * scale[...]).astype(LOW)
        k = qkv[:, share + at : share + at + size].astype(LOW)
        v = qkv[:, 2 * share + at : 2 * share + at + size].astype(LOW)
        own = whole[:, at : at + size]
        gq_parts, gk, gv = [], 0.0, 0.0
        for b in range(2):
            start, end = b * block, (b + 1) * block
            probs = probabilities(q[start:end], k[:end], start, info[1 + seq])
            grad_probs = nt(own[start:end], v[:end])
            delta = jnp.sum(grad_probs * probs, axis=-1, keepdims=True)
            grad_scores = (probs * (grad_probs - delta)).astype(LOW)
            gq_parts.append(nn(grad_scores, k[:end]))
            gk_new = tn(grad_scores, q[start:end])
            gv_new = tn(probs.astype(LOW), own[start:end])
            if b:
                gk = gk_new + jnp.concatenate([gk, jnp.zeros_like(gk)], 0)
                gv = gv_new + jnp.concatenate([gv, jnp.zeros_like(gv)], 0)
            else:
                gk, gv = gk_new, gv_new
        gq = jnp.concatenate(gq_parts, 0).astype(LOW).astype(WIDE)
        grad_scale = grad_scale + jnp.sum(gq * raw, axis=0, keepdims=True)
        grad_q.append(gq * scale[...])
        grad_k.append(gk)
        grad_v.append(gv)
    pad = jnp.zeros((total, w.shape[1] - 3 * share), WIDE)
    grads_all = jnp.concatenate(grad_q + grad_k + grad_v + [pad], 1).astype(LOW)
    partial = nt(grads_all, w[...])
    gain_grad = jnp.sum(partial * unit, axis=0, keepdims=True)
    scale_row = jnp.concatenate([grad_scale, jnp.zeros((1, width - size), WIDE)], 1)
    p_ref[...] = partial.astype(WIDE)
    for k in range(4):
        keep[k] = p_ref[pl.ds((2 * k + y) * rows, rows), :].astype(LOW)
        send[k] = p_ref[pl.ds((2 * k + 1 - y) * rows, rows), :].astype(LOW)
    result = tn(normed, grads_all)
    if not seq:
        grads[...] = result
        sums[...] = jnp.concatenate([gain_grad, scale_row, jnp.zeros((6, width), WIDE)], 0)
        return
    sums[...] = sums_before[...] + jnp.concatenate([gain_grad, scale_row, jnp.zeros((6, width), WIDE)], 0)
    g_ref[...] = result + before[...]
    c = info[4]
    piece = share // 4
    for t in range(8):
        for half in range(2):
            base = t * share + 2 * half * piece
            left[t, half] = g_ref[pl.ds(base + c * piece, piece), :].astype(LOW)
            right[t, half] = g_ref[pl.ds(base + (1 - c) * piece, piece), :].astype(LOW)


def feed_kernel(rows, info, att, tokens, cotangent, gains, *refs):
    blocks, refs = refs[:12], refs[12:]
    layer_out, grad_hidden_out, ga, left, keep, send, sums, w_out, w_up, w_down, sems = refs
    x, g = info[3], info[5]
    piece = blocks[0].shape[0]
    copies = []
    for j, w in enumerate((w_out, w_up, w_down)):
        for k in range(4):
            target = w.at[pl.ds(pl.multiple_of((g ^ k) * piece, piece), piece), :]
            copies.append(pltpu.make_async_copy(blocks[4 * j + k], target, sems.at[j, k]))
            copies[-1].start()

    def arrived(j):
        for k in range(4):
            copies[4 * j + k].wait()

    gain, bias_up, bias_down = gains[1:2], gains[2:3], gains[3:4]
    attended = jnp.concatenate([att[t] for t in range(8)], 1)
    wide = tokens[...].astype(WIDE)
    count, width = wide.shape
    arrived(0)
    hidden = wide + nn(attended, w_out[...])
    inv = lax.rsqrt(jnp.mean(hidden * hidden, axis=-1, keepdims=True) + EPS)
    normed = (hidden * inv * gain).astype(LOW)
    arrived(1)
    pre = nn(normed, w_up[...]) + bias_up
    sigma = jax.nn.sigmoid(pre)
    act = (pre * sigma).astype(LOW)
    arrived(2)
    layer_out[...] = (hidden + nn(act, w_down[...]) + bias_down).astype(LOW)
    row = lax.broadcasted_iota(jnp.int32, (count, 1), 0)
    at = info[6] * rows + jnp.where(row < rows, row, row - rows)
    valid = at < jnp.where(row < rows, info[1], info[2])
    grad_out = jnp.where(valid, cotangent[...].astype(WIDE), 0.0)
    grad_out_low = grad_out.astype(LOW)
    grad_act = nt(grad_out_low, w_down[...])
    grad_pre = (grad_act * sigma * (1.0 + pre * (1.0 - sigma))).astype(LOW)
    grad_normed = nt(grad_pre, w_up[...])
    weighted = grad_normed * gain
    grad_hidden = (
        grad_out
        + inv * weighted
        - hidden * (inv * inv * inv) * jnp.mean(weighted * hidden, axis=-1, keepdims=True)
    )
    grad_mixed = grad_hidden.astype(LOW)
    grad_hidden_out[...] = grad_hidden
    grad_att = nt(grad_mixed, w_out[...])
    share = ga.shape[-1]
    for t in range(8):
        ga[t] = grad_att[:, t * share : (t + 1) * share].astype(LOW)
    half = width // 2
    for j, (a, b) in enumerate(((attended, grad_mixed), (normed, grad_pre), (act, grad_out_low))):
        left[:, j * width : (j + 1) * width] = a
        first, second = b[:, :half], b[:, half:]
        keep[:, j * half : (j + 1) * half] = jnp.where(x == 0, first, second)
        send[:, j * half : (j + 1) * half] = jnp.where(x == 0, second, first)
    zeros = jnp.zeros((5, width), WIDE)
    sums[...] = jnp.concatenate(
        [
            jnp.sum(grad_normed * hidden * inv, axis=0, keepdims=True),
            jnp.sum(grad_pre.astype(WIDE), axis=0, keepdims=True),
            jnp.sum(grad_out, axis=0, keepdims=True),
            zeros,
        ],
        0,
    )


def weight_grad_kernel(info, *refs):
    lefts, rights, (keep, send, result) = refs[:4], refs[4:8], refs[8:]
    c, y = info[4], info[0]
    width = lefts[0].shape[1] // 3
    half = rights[0].shape[1] // 3
    quarter = half // 2
    for j in range(3):
        a = jnp.concatenate([r[:, j * width : (j + 1) * width] for r in lefts], 0)
        b = jnp.concatenate([r[:, j * half : (j + 1) * half] for r in rights], 0)
        b = jnp.where(c == 0, b[:, :quarter], b[:, quarter:])
        result[:, j * quarter : (j + 1) * quarter] = tn(a, b)
    share = width // 8
    for k in range(4):
        keep[k] = result[pl.ds((2 * k + y) * share, share), :].astype(LOW)
        send[k] = result[pl.ds((2 * k + 1 - y) * share, share), :].astype(LOW)


def add_z_kernel(info, keep, received, own, *sends):
    z = info[7]
    own[...] = keep[z].astype(WIDE) + received[z].astype(WIDE)
    for k, send in enumerate(sends):
        at = z ^ (k + 1)
        send[...] = (keep[at].astype(WIDE) + received[at].astype(WIDE)).astype(LOW)


def scatter_seq(info, keep, send):
    received = swap(send, "seq", 1, 8)
    part = keep.shape[1:]
    own, *sends = call(
        add_z_kernel,
        (shape(*part, dtype=WIDE), shape(*part), shape(*part), shape(*part)),
        [(info, SMEM), (keep, VMEM), (received, VMEM)],
    )
    return [own] + [swap(v, "seq", 2 * (k + 1), 8) for k, v in enumerate(sends)]


def add_all(parts):
    return sum(p.astype(WIDE) for p in parts[1:]) + parts[0]


def tokens_kernel(tokens, gain, grad_hidden, *refs):
    out, parts = refs[-1], refs[:-1]
    rows = out.shape[1]
    for seq in range(out.shape[0]):
        grad = parts[4 * seq][...]
        for part in parts[4 * seq + 1 : 4 * seq + 4]:
            grad = grad + part[...].astype(WIDE)
        wide = tokens[seq].astype(WIDE)
        inv = lax.rsqrt(jnp.mean(wide * wide, axis=-1, keepdims=True) + EPS)
        weighted = grad * gain[...]
        out[seq] = (
            grad_hidden[seq]
            + inv * weighted
            - wide * (inv * inv * inv) * jnp.mean(weighted * wide, axis=-1, keepdims=True)
        )


def columns_kernel(info, a, b, c, d, *outs):
    g = info[5]
    low, high = (g & 1) == 1, (g & 2) == 2
    pieces = [r[...].astype(WIDE) for r in (a, b, c, d)]
    half = [jnp.where(low, pieces[p ^ 1], pieces[p]) for p in range(4)]
    pieces = [jnp.where(high, half[p ^ 2], half[p]) for p in range(4)]
    quarter = a.shape[1] // 3
    for j, out in enumerate(outs):
        out[...] = jnp.concatenate([p[:, j * quarter : (j + 1) * quarter] for p in pieces], 1)


def rows_kernel(share, info, a, b, c, d, *outs):
    g = info[5]
    for k, piece in enumerate((a, b, c, d)):
        count = piece.shape[1]
        at = pl.ds(pl.multiple_of((g ^ k) * count, 8), count)
        for j, out in enumerate(outs):
            out[at, :] = jnp.concatenate(
                [piece[t, :, j * share : (j + 1) * share].astype(WIDE) for t in range(8)], 1
            )


def payload_kernel(a, b, c, smalls, out):
    share = a.shape[1] // 8
    for t in range(8):
        cols = [r[:, t * share : (t + 1) * share].astype(WIDE) for r in (a, b, c)]
        out[t] = jnp.concatenate(cols + [smalls[...]], 1).astype(LOW)


def quick(
    tokens,
    lengths,
    query_weight,
    key_weight,
    value_weight,
    out_weight,
    up_weight,
    down_weight,
    norm_gain,
    ff_gain,
    up_bias,
    down_bias,
    query_scale,
    cotangent,
):
    seq_count, rows, width = tokens.shape
    size = query_scale.shape[0]
    share = width // 8
    count = seq_count * rows
    wide_cols = -(-(3 * share + 4) // 128) * 128
    wrows = query_weight.shape[0]
    g, s = lax.axis_index("grp"), lax.axis_index("seq")
    x, c, z, y = g // 2, g % 2, s // 2, s % 2
    info = jnp.stack([y, lengths[0], lengths[1], x, c, g, s, z]).astype(jnp.int32)

    smalls = jnp.stack([norm_gain, ff_gain, up_bias, down_bias], 1).astype(WIDE)
    smalls = jnp.pad(smalls, ((0, 0), (0, wide_cols - 3 * share - 4)))
    payload = call(
        payload_kernel,
        shape(8, wrows, wide_cols),
        [(query_weight, VMEM), (key_weight, VMEM), (value_weight, VMEM), (smalls, VMEM)],
    )
    columns = lax.all_to_all(payload, "seq", 0, 0, tiled=True)
    mine = over_z(tokens, z)
    other = swap(mine, "seq", 1, 8)
    w_qkv = jnp.stack(in_order(over_grp(columns), g)).reshape(width, wide_cols)
    gains = w_qkv[:, 3 * share : 3 * share + 4].T.astype(WIDE)
    gain_one = gains[0:1]
    blocks = []
    for w in (out_weight, up_weight, down_weight):
        blocks += [v.reshape(8 * wrows, width) for v in over_grp(gather_seq(w, z, y))]
    factor = QCONST / math.sqrt(size)
    scale = (factor * jax.nn.softplus(query_scale)).reshape(1, size)

    att = call(
        functools.partial(attend_kernel, size),
        shape(8, seq_count, rows, share),
        [(info, SMEM), (mine, VMEM), (other, VMEM), (w_qkv, VMEM), (gain_one, VMEM), (scale, VMEM)],
        [pltpu.VMEM((8 * rows, width), LOW)],
        flops=2 * seq_count * 8 * rows * width * wide_cols,
    )
    att = lax.all_to_all(att, "seq", 0, 0, tiled=True).reshape(8, count, share)

    layer_out, grad_hidden, grad_att, left, keep, send, sums_ff = call(
        functools.partial(feed_kernel, rows),
        (
            shape(count, width),
            shape(count, width, dtype=WIDE),
            shape(8, count, share),
            shape(count, 3 * width),
            shape(count, 3 * width // 2),
            shape(count, 3 * width // 2),
            shape(8, width, dtype=WIDE),
        ),
        [
            (info, SMEM),
            (att, VMEM),
            (tokens.reshape(count, width), VMEM),
            (cotangent.reshape(count, width), VMEM),
            (gains, VMEM),
        ]
        + [(b, ANY) for b in blocks],
        [pltpu.VMEM((width, width), LOW)] * 3 + [pltpu.SemaphoreType.DMA((3, 4))],
        flops=14 * count * width * width,
    )
    grad_att = lax.all_to_all(grad_att, "seq", 0, 0, tiled=True).reshape(8, seq_count, rows, share)

    lefts = over_grp(left)
    far = swap(send, "grp", 2, 4)
    rights = [keep, swap(keep, "grp", 1, 4), far, swap(far, "grp", 1, 4)]
    keep, send = call(
        weight_grad_kernel,
        (shape(4, share, 3 * width // 4), shape(4, share, 3 * width // 4)),
        [(info, SMEM)] + [(v, VMEM) for v in lefts + rights],
        [pltpu.VMEM((width, 3 * width // 4), WIDE)],
        flops=6 * 4 * count * width * width // 4,
    )
    ff_part = add_all(scatter_seq(info, keep, send)).astype(LOW)
    whole = shape(share, width, dtype=WIDE)
    ff_grads = call(
        columns_kernel, (whole, whole, whole), [(info, SMEM)] + [(v, VMEM) for v in over_grp(ff_part)]
    )

    parts, carried = [], []
    for seq in range(seq_count):
        scratch = [pltpu.VMEM((8 * rows, width), LOW), pltpu.VMEM((8 * rows, width), WIDE)]
        outs = [shape(4, rows, width), shape(4, rows, width)]
        if seq:
            scratch.append(pltpu.VMEM((width, wide_cols), WIDE))
            outs += [shape(8, 2, wrows, wide_cols), shape(8, 2, wrows, wide_cols)]
        else:
            outs.append(shape(width, wide_cols, dtype=WIDE))
        keep, send, *carried = call(
            functools.partial(attend_back_kernel, size, seq),
            tuple(outs) + (shape(8, width, dtype=WIDE),),
            [(info, SMEM), (mine, VMEM), (other, VMEM), (w_qkv, VMEM), (gain_one, VMEM), (scale, VMEM)]
            + [(grad_att, VMEM)]
            + [(v, VMEM) for v in carried],
            scratch,
            flops=6 * 8 * rows * width * wide_cols,
        )
        parts += scatter_seq(info, keep, send)
    half_keep, half_send, sums_att = carried
    grad_tokens = call(
        tokens_kernel,
        shape(seq_count, rows, width, dtype=WIDE),
        [(tokens, VMEM), (gain_one, VMEM), (grad_hidden.reshape(seq_count, rows, width), VMEM)]
        + [(v, VMEM) for v in parts],
    )

    half = half_keep.astype(WIDE) + swap(half_send, "grp", 1, 4).astype(WIDE)
    part = lax.dynamic_index_in_dim(half, x, 1, keepdims=False)
    far = lax.dynamic_index_in_dim(half, 1 - x, 1, keepdims=False).astype(LOW)
    part = part + swap(far, "grp", 2, 4).astype(WIDE)
    part = lax.all_to_all(part.astype(LOW), "seq", 0, 0, tiled=True)
    qkv_grads = call(
        functools.partial(rows_kernel, share),
        (whole, whole, whole),
        [(info, SMEM)] + [(v, VMEM) for v in over_grp(part)],
    )

    sums = jnp.concatenate([sums_att[:2], sums_ff[:3], sums_ff[5:8]], 0)
    for axis, bit, length in (("grp", 1, 4), ("grp", 2, 4), ("seq", 1, 8), ("seq", 2, 8), ("seq", 4, 8)):
        sums = sums + swap(sums, axis, bit, length)
    grad_scale = sums[1, :size] * factor * jax.nn.sigmoid(query_scale)
    return (
        layer_out.reshape(seq_count, rows, width),
        grad_tokens,
        *qkv_grads,
        *ff_grads,
        sums[0],
        sums[2],
        sums[3],
        sums[4],
        grad_scale,
    )


def solution(mesh):
    fits = mesh.shape["grp"] == 4 and mesh.shape["seq"] == 8
    return jax.shard_map(
        quick if fits else shards,
        mesh=mesh,
        in_specs=(
            P("grp", "seq", None),
            P("grp"),
            P(("grp", "seq"), None),
            P(("grp", "seq"), None),
            P(("grp", "seq"), None),
            P(("grp", "seq"), None),
            P(("grp", "seq"), None),
            P(("grp", "seq"), None),
            P(("grp", "seq")),
            P(("grp", "seq")),
            P(("grp", "seq")),
            P(("grp", "seq")),
            P(),
            P("grp", "seq", None),
        ),
        out_specs=(
            P("grp", "seq", None),
            P("grp", "seq", None),
            P("seq", None),
            P("seq", None),
            P("seq", None),
            P("seq", None),
            P("seq", None),
            P("seq", None),
            P(),
            P(),
            P(),
            P(),
            P(),
        ),
        check_vma=False,
    )
```
